32 devices in a mesh: dev: 32 (over z, y, x, core).
Axes of the slice: x: 2, y: 2, z: 4, core: 2. Of those that a mesh axis runs over, the one named last changes fastest.
Arguments:
- planes: bfloat16 [128, 19, 19, 17], P('dev'), may hold values from 0 to 1, as said below
- history: int32 [128, 8], P('dev'), may hold values from 0 to 1, as said below
- stem_kernel: bfloat16 [39168], P('dev'), may hold values from -0.5 to 0.5
- stem_gain: bfloat16 [256], P('dev'), may hold values from 0.5 to 1.5
- stem_shift: bfloat16 [256], P('dev'), may hold values from -3 to 3
- first_kernel: bfloat16 [589824], P('dev'), may hold values from -0.125 to 0.125
- first_gain: bfloat16 [256], P('dev'), may hold values from 0.5 to 1.5
- first_shift: bfloat16 [256], P('dev'), may hold values from -3 to 3
- second_kernel: bfloat16 [589824], P('dev'), may hold values from -0.125 to 0.125
- second_gain: bfloat16 [256], P('dev'), may hold values from 0.5 to 1.5
- second_shift: bfloat16 [256], P('dev'), may hold values from -3 to 3
- cotangent: bfloat16 [128, 19, 19, 256], P('dev'), may hold values from -6 to 6
Outputs:
- activations: bfloat16 [128, 19, 19, 256], P('dev')
- planes_grad: float32 [128, 19, 19, 17], P('dev')
- stem_kernel_grad: float32 [39168], P('dev')
- stem_gain_grad: float32 [256], P('dev')
- stem_shift_grad: float32 [256], P('dev')
- first_kernel_grad: float32 [589824], P('dev')
- first_gain_grad: float32 [256], P('dev')
- first_shift_grad: float32 [256], P('dev')
- second_kernel_grad: float32 [589824], P('dev')
- second_gain_grad: float32 [256], P('dev')
- second_shift_grad: float32 [256], P('dev')
The draws below stay inside these ranges and needn't reach their ends.
Inputs may be any that keep to these rules, and one draw needn't show every extreme that they name: `planes`: each entry is 0 or 1; the last plane is constant over a position's squares. The available history slots of a position are its first ones; the first slot is always available.
All inputs are finite; a program needn't handle non-finite values.
Results may differ from the reference program's by a relative error of at most 0.0075.
Values may be sent and summed in bfloat16 or wider, within the bound.
A program may use at most 128 MiB of HBM per device.

```python
import jax
import jax.numpy as jnp
from jax import lax

C = 256
PLANES = 17
HISTORY = 8
BOARD = 19
POSITIONS = 128


def draw_planes(key, part):
    key = jax.random.fold_in(key, 5)
    stone_key, colour_key = jax.random.split(key)
    stones = jax.random.bernoulli(stone_key, 0.35, (POSITIONS, BOARD, BOARD, PLANES - 1)).astype(jnp.float32)
    colour = jax.random.bernoulli(colour_key, 0.5, (POSITIONS, 1, 1, 1)).astype(jnp.float32)
    colour = jnp.broadcast_to(colour, (POSITIONS, BOARD, BOARD, 1))
    return jnp.concatenate([stones, colour], axis=3).astype(jnp.bfloat16)


def draw_history(key, part):
    key = jax.random.fold_in(key, 11)
    position_ids = jnp.arange(POSITIONS, dtype=jnp.int32)
    upper_bound = 1 + HISTORY * position_ids // POSITIONS
    available = jax.random.randint(key, (POSITIONS,), 1, upper_bound + 1)
    slot_ids = jnp.arange(HISTORY, dtype=jnp.int32)
    return (slot_ids[None, :] < available[:, None]).astype(jnp.int32)


def levels(rng, dims, cuts, least, high):
    factor_of, own = 1.0, jax.random.fold_in(rng, 6)
    for position, parts in cuts:
        heights = jnp.exp(jax.random.uniform(jax.random.fold_in(own, position), (parts,), jnp.float32, least / len(cuts), high / len(cuts)))
        factor_of = factor_of * jnp.repeat(heights, dims[position] // parts).reshape([-1 if axis == position else 1 for axis in range(len(dims))])
    return factor_of


def centred(key, shape, scale, most, shards=(), kind=jnp.bfloat16):
    array = jax.random.normal(key, shape, jnp.float32) * scale
    if len(shards) > 0:
        array = levels(key, shape, shards, -0.22, 0.18) * array
    return jnp.clip(array, min=-most, max=most).astype(kind)


def setup_inputs(seed: int = 0) -> dict:
    streams_of = jax.random.split(jax.random.key(seed), 13)
    return {
        "planes": draw_planes(jax.random.fold_in(streams_of[12], 71), 0),
        "history": draw_history(jax.random.fold_in(streams_of[12], 71), 0),
        "stem_kernel": centred(streams_of[2], (9 * PLANES * C,), (9 * PLANES) ** -0.5, 0.5, ((0, 32),)),
        "stem_gain": jnp.clip(0.5 + 1.0 * jax.random.uniform(streams_of[3], (C,), jnp.float32) ** levels(streams_of[3], (C,), ((0, 32),), -0.2, 0.2), 0.5, 1.5).astype(jnp.bfloat16),
        "stem_shift": centred(streams_of[4], (C,), 0.5, 3.0, ((0, 32),)),
        "first_kernel": centred(streams_of[5], (9 * C * C,), (9 * C) ** -0.5, 0.125, ((0, 32),)),
        "first_gain": jnp.clip(0.5 + 1.0 * jax.random.uniform(streams_of[6], (C,), jnp.float32) ** levels(streams_of[6], (C,), ((0, 32),), -0.2, 0.2), 0.5, 1.5).astype(jnp.bfloat16),
        "first_shift": centred(streams_of[7], (C,), 0.5, 3.0, ((0, 32),)),
        "second_kernel": centred(streams_of[8], (9 * C * C,), (9 * C) ** -0.5, 0.125, ((0, 32),)),
        "second_gain": jnp.clip(0.5 + 1.0 * jax.random.uniform(streams_of[9], (C,), jnp.float32) ** levels(streams_of[9], (C,), ((0, 32),), -0.2, 0.2), 0.5, 1.5).astype(jnp.bfloat16),
        "second_shift": centred(streams_of[10], (C,), 0.5, 3.0, ((0, 32),)),
        "cotangent": centred(streams_of[11], (POSITIONS, BOARD, BOARD, C), 1.0, 6.0, ((0, 32),)),
    }


epsilon = 1e-05

@jax.custom_vjp
def low(v):
    return lax.optimization_barrier(v.astype(jnp.bfloat16)).astype(jnp.float32)

@jax.custom_vjp
def low_back(v):
    return v

def low_keep(v):
    return (low(v), None)

def low_pass(kept, grad):
    return (grad,)

def back_keep(v):
    return (v, None)

def back_low(kept, grad):
    return (low(grad),)
low.defvjp(low_keep, low_pass)
low_back.defvjp(back_keep, back_low)

def swish(value):
    return value * jax.nn.sigmoid(value)

def convolve(source, kernel):
    return lax.conv_general_dilated(source, kernel, (1, 1), 'SAME', dimension_numbers=('NHWC', 'HWIO', 'NHWC'), precision=lax.Precision.HIGHEST)

def normalize(pre_value, gain_all, shift_all):
    centre = lax.optimization_barrier(jnp.mean(pre_value, axis=(0, 1, 2)))
    variance = lax.optimization_barrier(jnp.mean(pre_value * pre_value, axis=(0, 1, 2))) - centre * centre
    return (pre_value - centre) * lax.rsqrt(variance + epsilon) * gain_all + shift_all

def reference(planes, history, stem_kernel, stem_gain, stem_shift, first_kernel, first_gain, first_shift, second_kernel, second_gain, second_shift, cotangent):
    present = jnp.concatenate([jnp.repeat(history, 2, axis=1), jnp.ones((history.shape[0], 1), jnp.int32)], axis=1).astype(jnp.float32)[:, None, None, :]

    def forward(plane_values, stem_weight, stem_scale, stem_offset, first_weight, first_scale, first_offset, second_weight, second_scale, second_offset):
        channels = stem_scale.shape[0]
        stem_pre = low_back(convolve(plane_values * present, stem_weight.reshape(3, 3, plane_values.shape[3], channels)))
        stem_act = low(swish(normalize(stem_pre, stem_scale, stem_offset)))
        first_pre = low_back(convolve(stem_act, first_weight.reshape(3, 3, channels, channels)))
        first_act = low(swish(normalize(first_pre, first_scale, first_offset)))
        second_pre = low_back(convolve(first_act, second_weight.reshape(3, 3, channels, channels)))
        return swish(normalize(second_pre, second_scale, second_offset) + stem_act)
    activations, pullback = jax.vjp(forward, planes.astype(jnp.float32), stem_kernel.astype(jnp.float32), stem_gain.astype(jnp.float32), stem_shift.astype(jnp.float32), first_kernel.astype(jnp.float32), first_gain.astype(jnp.float32), first_shift.astype(jnp.float32), second_kernel.astype(jnp.float32), second_gain.astype(jnp.float32), second_shift.astype(jnp.float32))
    grads = pullback(cotangent.astype(jnp.float32))
    return (activations.astype(jnp.bfloat16), grads[0], grads[1], grads[2], grads[3], grads[4], grads[5], grads[6], grads[7], grads[8], grads[9])
```

```python
import functools
import math

import jax
import jax.numpy as jnp
from jax import lax
from jax.experimental import pallas as pl
from jax.experimental.pallas import tpu as pltpu
from jax.sharding import PartitionSpec as P

F32 = jnp.float32
BF16 = jnp.bfloat16
MESH = pl.DeviceIdType.MESH
EPSILON = 1e-5
GROUP = 8
QUAD = GROUP // 2


def up(value, step):
    return -(-value // step) * step


class Sizes:
    def __init__(self, n, planes_t, cot_t, stem_len, kernel_len):
        self.n = n
        self.outer = n // GROUP
        self.board, self.planes, self.pos, _ = planes_t
        self.channels = cot_t[3]
        self.block = (self.board + 1) * self.pos
        self.live = self.board * self.pos
        self.rows = self.board * self.block
        self.deep = up(self.rows, 128)
        self.tall = 2 * self.block + self.deep
        self.taps = 9
        self.width = 256
        self.stem_len = stem_len
        self.stem_apart = 2 * stem_len >= 7 * self.channels
        self.stem_all = up(n * stem_len // self.channels, 8) + 8
        self.krows = kernel_len // self.channels
        self.kmsg = up(2 * self.krows + 4, 16)
        self.gmsg = up(2 * self.krows, 16)
        self.vec = self.channels // n
        self.first_row = up(2 * self.krows, 8)
        self.stem_row = 2 * self.first_row
        self.vec_row = self.stem_row + 16
        self.packed = self.vec_row + 8
        self.cells = n * self.pos * self.board * self.board


def iota(shape, axis):
    return lax.broadcasted_iota(jnp.int32, shape, axis)


def wait_bytes(ref, sem):
    pltpu.make_async_copy(ref, ref, sem).wait()


def dot(a, b):
    return lax.dot_general(a, b, (((1,), (0,)), ((), ())), preferred_element_type=F32)


def dot_nt(a, b):
    return lax.dot_general(a, b, (((1,), (1,)), ((), ())), preferred_element_type=F32)


def dot_tn(a, b):
    return lax.dot_general(a, b, (((0,), (0,)), ((), ())), preferred_element_type=F32)


def kernel(
    z_,
    planes_hbm, cot_hbm, hist_h, stem_kh, stem_gh, stem_sh, first_kh, first_gh, first_sh, second_kh, second_gh, second_sh,
    act_hbm, pgrad_hbm, packed,
    hist, stem_k, stem_g, stem_s, first_k, first_g, first_s, second_k, second_g, second_s,
    planes_v, cot_v, act_v, pgrad_v, y_f, vm, e_mat, s_in, s_t, k0, k0f, wtx, w1, w2, wt1, wt2,
    x0, x1, xp, h0, h1, h2, sl0, sl1, g2, big, pre_t, tmp,
    sbuf, kbuf1, kbuf2, ar_a,
    dk1, dk2, rc1, rc2, rx1, rx2, ry1, ry2, rz1, rz2, rw1, rw2,
    dk0, rw0,
    loc, sm_s, sm_r, kg_s, kg_r, ar_s, ar_r, rs_s, rs_r,
):
    n, outer, c_all = z_.n, z_.outer, z_.channels
    block, live, rows, deep = z_.block, z_.live, z_.rows, z_.deep
    board, pos, planes = z_.board, z_.pos, z_.planes
    me = lax.axis_index("dev")
    zi = me // GROUP
    ii = me % GROUP
    qi = ii // 2
    ci = ii % 2

    def dev(o, i):
        return o * GROUP + i

    def remote(src, dst, send, recv, target):
        copy = pltpu.make_async_remote_copy(
            src_ref=src, dst_ref=dst, send_sem=send, recv_sem=recv, device_id=(target,), device_id_type=MESH
        )
        copy.start()

    bits = n.bit_length() - 1
    steps = [(1 - 2 * (me // 2**b % 2)) * 2**b for b in range(bits)]

    def everyone(visit):
        for p in range(n - 1, 0, -1):
            visit(me + sum(steps[b] for b in range(bits) if p // 2**b % 2))

    outer_peers = [lax.rem(zi + k, outer) for k in range(1, outer)]
    inner_peers = [lax.rem(ii + k, GROUP) for k in range(1, GROUP)]
    quad_peers = [lax.rem(qi + k, QUAD) for k in range(1, QUAD)]
    sibling = dev(zi, qi * 2 + (1 - ci))

    loads = []
    for k, (src, dst) in enumerate((
        (stem_kh, stem_k), (stem_gh, stem_g), (stem_sh, stem_s), (first_kh, first_k), (first_gh, first_g),
        (first_sh, first_s), (second_kh, second_k), (second_gh, second_g), (second_sh, second_s), (hist_h, hist),
    )):
        copy = pltpu.make_async_copy(src, dst, loc.at[4 + k])
        copy.start()
        loads.append(copy)
    load_planes = pltpu.make_async_copy(planes_hbm, planes_v, loc.at[0])
    load_planes.start()
    load_cot = pltpu.make_async_copy(cot_hbm, cot_v, loc.at[1])
    load_cot.start()
    barrier = pltpu.get_barrier_semaphore()

    def greet(other):
        pl.semaphore_signal(barrier, inc=1, device_id=(other,), device_id_type=MESH)

    for o in outer_peers:
        greet(dev(o, ii))
    for i in inner_peers:
        greet(dev(zi, i))
    for copy in loads:
        copy.wait()
    lane = iota((16, 128), 1)
    row = iota((16, 128), 0)

    def placed(vec_ref, slot):
        tmp[0:8, :] = jnp.zeros((8, 128), F32)
        tmp[0:1, 0 : z_.vec] = vec_ref[...].astype(F32)
        start = me * z_.vec
        spread = pltpu.roll(tmp[0:8, :], lax.rem(start, 128), 1)[0:1, :]
        return jnp.where(row == slot + start // 128, spread, 0.0)

    length = z_.stem_len
    off = lax.rem(me * length, c_all)
    tmp[0:16, :] = jnp.zeros((16, 128), F32)
    for r in range(length // 128):
        tmp[r : r + 1, :] = stem_k[pl.ds(128 * r, 128)].astype(F32).reshape(1, 128)
    rest = length % 128
    if rest:
        r = length // 128
        tmp[r : r + 1, 0:rest] = stem_k[pl.ds(128 * r, rest)].astype(F32).reshape(1, rest)
    shift = lax.rem(off, 128)
    rolled = pltpu.roll(tmp[0:16, :], shift, 1)
    flat = jnp.where(lane >= shift, rolled, pltpu.roll(rolled, 1, 0))
    flat = jnp.where(off // 128 == 1, pltpu.roll(flat, 1, 0), flat)
    tmp[0:16, :] = flat
    left = tmp[pl.ds(0, 8, stride=2), :]
    right = tmp[pl.ds(1, 8, stride=2), :]
    vectors = placed(stem_g, 12) + placed(stem_s, 14)
    tmp[0:16, :] = vectors
    tmp[0:6, :] = left[0:6, :]
    tmp[6:12, :] = right[0:6, :]
    sbuf[zi, ii] = tmp[0:16, :].astype(BF16)

    kr = z_.krows

    def kernel_message(k_ref, g_ref, s_ref, buf):
        vectors = placed(g_ref, 0) + placed(s_ref, 2)
        tmp[0 : 2 * kr, :] = k_ref[...].astype(F32)
        left = tmp[pl.ds(0, kr, stride=2), :]
        right = tmp[pl.ds(1, kr, stride=2), :]
        tmp[0:kr, :] = left
        tmp[kr : 2 * kr, :] = right
        tmp[2 * kr : 2 * kr + 16, :] = vectors
        buf[zi, qi, ci] = tmp[0 : z_.kmsg, :].astype(BF16)

    kernel_message(first_k, first_g, first_s, kbuf1)

    def gather_near(g, block_o, o):
        for q in quad_peers:
            remote(block_o, block_o, kg_s.at[g, 1], kg_r.at[g, 1, o], dev(zi, q * 2 + ci))

    def gather_begin(g, buf):
        mine = buf.at[zi, qi, ci]
        for o in outer_peers:
            remote(mine, mine, kg_s.at[g, 0], kg_r.at[g, 0, zi], dev(o, ii))
        gather_near(g, mine, zi)

    def gather_quad(g, buf):
        for o in outer_peers:
            block_o = buf.at[o, qi, ci]
            wait_bytes(block_o, kg_r.at[g, 0, o])
            gather_near(g, block_o, o)

    def gather_core(g, buf, which):
        for o in which:
            wait_bytes(buf.at[o, pl.ds(0, QUAD - 1), 0], kg_r.at[g, 1, o])
            remote(buf.at[o, :, ci], buf.at[o, :, ci], kg_s.at[g, 2], kg_r.at[g, 2, o], sibling)

    def gather_end(g, buf, w):
        many = 16 // math.gcd(16, kr)

        def place(p, vectors):
            there = w.at[pl.ds(pl.multiple_of(p * many * kr, 16), many * kr)]
            for d in range(many):
                s = p * many + d
                piece = buf.at[s // GROUP, (s % GROUP) // 2, s % 2]
                there[kr * d : kr * d + kr, 0:128] = piece[0:kr, :]
                there[kr * d : kr * d + kr, 128:256] = piece[kr : 2 * kr, :]
                vectors += piece[2 * kr : z_.kmsg, :].astype(F32)[0:4, :]
            return vectors

        vectors = jnp.zeros((4, 128), F32)
        for o in [zi] + outer_peers:
            wait_bytes(buf.at[o, :, 0], kg_r.at[g, 2, o])
            each = GROUP // many
            for p in range(each):
                vectors = place(o * each + p, vectors)
        return wide(vectors[0:2, :]), wide(vectors[2:4, :])

    def wide(two_rows):
        return jnp.concatenate([two_rows[0:1, :], two_rows[1:2, :]], axis=1)

    pl.semaphore_wait(barrier, outer - 1 + GROUP - 1)
    for o in outer_peers:
        remote(sbuf.at[zi, ii], sbuf.at[zi, ii], sm_s.at[0], sm_r.at[0], dev(o, ii))
    gather_begin(0, kbuf1)

    load_planes.wait()
    for i in range(board):
        y_f[i * 128 : i * 128 + 128, :] = jnp.zeros((128, 128), F32)
        for k in range(planes):
            y_f[i * 128 + pos * k : i * 128 + pos * k + pos, 0:board] = planes_v[i, k].astype(F32)
    rep = (iota((block, 128), 0) // pos == iota((block, 128), 1)).astype(BF16)
    tmp[0:8, :] = jnp.zeros((8, 128), F32)
    tmp[0:pos, 0:8] = hist[...].astype(F32)
    spread = (iota((128, 128), 1) // (2 * pos) == iota((128, 128), 0)).astype(BF16)
    present = dot(tmp[0:8, :].astype(BF16), spread)
    lane8 = iota((8, 128), 1)
    present = jnp.where(lane8 // pos == planes - 1, 1.0, present)
    present = jnp.sum(jnp.where((lane8 % pos == iota((8, 128), 0)) & (lane8 < planes * pos), present, 0.0), axis=0, keepdims=True)
    lane_b = iota((block, 128), 1)
    pick = jnp.where(lane_b % pos == iota((block, 128), 0) % pos, present, 0.0)
    wider = (iota((128, 128), 1) // pos == iota((128, 128), 0)).astype(BF16)
    for m in range(0, board, 5):
        count = min(5, board - m)
        spread_t = dot(y_f[m * 128 : (m + count) * 128, :].astype(BF16), wider)
        for i in range(count):
            v = jnp.transpose(spread_t[i * 128 : i * 128 + 128, :])[0:block, :] * pick
            at = slice((m + i + 1) * block, (m + i + 2) * block)
            vm[0, at, :] = pltpu.roll(v, pos, 0).astype(BF16)
            vm[1, at, :] = v.astype(BF16)
            vm[2, at, :] = pltpu.roll(v, block - pos, 0).astype(BF16)

    wait_bytes(sbuf.at[pl.ds(0, outer - 1), 0], sm_r.at[0])
    for i in inner_peers:
        remote(sbuf.at[:, ii], sbuf.at[:, ii], sm_s.at[1], sm_r.at[1], dev(zi, i))
    gather_quad(0, kbuf1)
    kernel_message(second_k, second_g, second_s, kbuf2)
    gather_begin(1, kbuf2)

    for b in range(3):
        vm[b, 0:block, :] = jnp.zeros((block, 128), BF16)
        vm[b, block + rows :, :] = jnp.zeros((z_.tall - block - rows, 128), BF16)
    for t in range(9):
        er = iota((128, z_.width), 0)
        e_mat[128 * t : 128 * t + 128, :] = (
            (iota((128, z_.width), 1) == planes * t + er // pos) & (er < planes * pos)
        ).astype(BF16)

    cuts = [0] + [min(m, board) for m in range(3, board, 6)] + [board]
    tiles = [(m, end - m) for m, end in zip(cuts, cuts[1:])]

    def taps(x, start, count):
        return jnp.concatenate([x[t % 3, start + (t // 3) * block : start + (t // 3) * block + count, :] for t in range(9)], axis=1)

    for m, count in tiles:
        s_in[m * block : (m + count) * block, :] = dot(taps(vm, m * block, count * block), e_mat[...]).astype(BF16)
    gather_core(0, kbuf1, [zi])

    k0f[...] = jnp.zeros(k0f.shape, F32)

    for x in (x0, x1, xp):
        for b in range(3):
            x[b, 0:block, :] = jnp.zeros((block, c_all), BF16)
            x[b, block + rows :, :] = jnp.zeros((z_.tall - block - rows, c_all), BF16)

    wait_bytes(sbuf.at[:, pl.ds(0, GROUP - 1)], sm_r.at[1])
    vectors = jnp.zeros((4, 128), F32)
    for s in range(n):
        piece = sbuf[s // GROUP, s % GROUP].astype(F32)
        base = s * length // c_all
        apart = s % 2 if z_.stem_apart else 0
        if z_.stem_apart:
            k0f[apart, base : base + 6, 0:128] = piece[0:6, :]
            k0f[apart, base : base + 6, 128:256] = piece[6:12, :]
        else:
            k0f[0, base : base + 6, 0:128] += piece[0:6, :]
            k0f[0, base : base + 6, 128:256] += piece[6:12, :]
        vectors += piece[12:16, :]
    gain0, shift0 = wide(vectors[0:2, :]), wide(vectors[2:4, :])
    k0[...] = jnp.zeros(k0.shape, BF16)
    used = up(9 * planes, 16)
    k0[0:used, :] = (k0f[0, 0:used, :] + k0f[1, 0:used, :]).astype(BF16)

    blk_mask = iota((block, c_all), 0) < live

    def fold(v):
        return jnp.sum(v.reshape(block // 8, 8, c_all), axis=0)

    def part(i, ahead=0):
        return slice((i + ahead) * block, (i + ahead + 1) * block)

    class Sums:
        def __init__(self):
            self.a = self.b = None

        def add(self, a, b):
            a, b = fold(a), fold(b)
            self.a = a if self.a is None else self.a + a
            self.b = b if self.b is None else self.b + b

        def rows(self):
            return jnp.sum(self.a, axis=0, keepdims=True), jnp.sum(self.b, axis=0, keepdims=True)

    def phase(x, w, produce, consume, between=None, before=None, whole=False):
        done = 0
        if before is not None:
            for i in range(board):
                produce(i)
            done = board
            before()
        for k, (m, count) in enumerate(tiles):
            upto = min(board, m + count + 1)
            for i in range(done, upto):
                produce(i)
            done = max(done, upto)
            out = dot(taps(x, m * block, count * block), w[...])
            if k + 1 < len(tiles):
                upto = min(board, tiles[k + 1][0] + tiles[k + 1][1] + 1)
                for i in range(done, upto):
                    produce(i)
                done = max(done, upto)
            if whole:
                consume(m, count, out)
            else:
                for i in range(count):
                    consume(m + i, out[i * block : (i + 1) * block, :])
            if between is not None:
                between(k)

    def reduce_begin(k, a, b):
        mine = ar_a.at[k, me]
        mine[0:1, :] = a[:, 0:128]
        mine[1:2, :] = a[:, 128:256]
        mine[2:3, :] = b[:, 0:128]
        mine[3:4, :] = b[:, 128:256]

        everyone(lambda other: remote(mine, mine, ar_s.at[k], ar_r.at[k], other))

    def reduce_end(k):
        wait_bytes(ar_a.at[k, pl.ds(0, n - 1)], ar_r.at[k])
        total = jnp.sum(ar_a[k], axis=0)
        return wide(total[0:2, :]), wide(total[2:4, :])

    def bn(total, squares, gain, shift):
        centre = total * (1.0 / z_.cells)
        variance = squares * (1.0 / z_.cells) - centre * centre
        inv = lax.rsqrt(variance + EPSILON)
        scale = gain * inv
        return inv, -centre * inv, scale, shift - centre * scale

    def put(x, i, v):
        at = part(i, 1)
        x[0, at, :] = pltpu.roll(v, pos, 0).astype(BF16)
        x[1, at, :] = v.astype(BF16)
        x[2, at, :] = pltpu.roll(v, block - pos, 0).astype(BF16)

    def activation(h, x, slope, stats):
        _, _, scale, bias = stats

        def produce(i):
            v = h[part(i), :] * scale + bias
            sig = 0.5 * jnp.tanh(0.5 * v) + 0.5
            act = v * sig
            slope[part(i), :] = jnp.where(blk_mask, sig + act * (1.0 - sig), 0.0)
            put(x, i, jnp.where(blk_mask, act, 0.0))

        return produce

    def keep_moments(h, total):
        def consume(i, out):
            h[part(i), :] = out
            v = jnp.where(blk_mask, out, 0.0)
            total.add(v, v * v)

        return consume

    def pre_gradient(g, h, stats, shift_grad, gain_grad, flip=True):
        inv, neg, scale, _ = stats
        a = shift_grad * (1.0 / z_.cells)
        b = gain_grad * (1.0 / z_.cells)
        flipped = [0]

        def produce(i):
            normed = h[part(i), :] * inv + neg
            v = scale * (g[part(i), :] - a - normed * b)
            put(xp, i, jnp.where(blk_mask, v, 0.0))
            if not flip:
                return
            upto = (i + 1) * block // 128 if i + 1 < board else deep // 128
            for k in range(flipped[0], upto):
                pre_t[:, 128 * k : 128 * k + 128] = jnp.transpose(xp[1, block + 128 * k : block + 128 * k + 128, :])
            flipped[0] = upto

        return produce

    def kernel_grad(x, dk, after):
        for t in range(9):
            o = dot(pre_t[...], x[t % 3, (t // 3) * block : (t // 3) * block + deep, :])
            o = jnp.transpose(o)
            r = 256 * t
            while r < 256 * t + 256:
                s, inner = r // kr, r % kr
                count = min(kr - inner, 256 * t + 256 - r)
                rows_o = o[r - 256 * t : r - 256 * t + count, :].astype(BF16)
                here = dk.at[s // GROUP, (s % GROUP) // 2, s % 2]
                here[inner : inner + count, :] = rows_o[:, 0:128]
                here[kr + inner : kr + inner + count, :] = rows_o[:, 128:256]
                r += count
            after(t)

    def transpose_weights(w, wt):
        for t in range(9):
            wt[256 * t : 256 * t + 256, :] = jnp.transpose(w[256 * (8 - t) : 256 * (8 - t) + 256, :])

    def scatter_core(k, dk, rc, which):
        for o in which:
            remote(dk.at[o, :, 1 - ci], rc.at[o], rs_s.at[k, 0], rs_r.at[k, 0, o], sibling)

    def scatter_quad(k, dk, rc, rx, ry, which):
        for o in which:
            wait_bytes(rc.at[o], rs_r.at[k, 0, o])
            for q in range(QUAD):
                rx[o, q] = (dk[o, q, ci].astype(F32) + rc[o, q].astype(F32)).astype(BF16)
            for q in quad_peers:
                remote(rx.at[o, q], ry.at[o, qi], rs_s.at[k, 1], rs_r.at[k, 1, o], dev(zi, q * 2 + ci))

    def scatter_begin(k, dk, rc, rx, ry):
        def complete(t):
            return range(256 * t // (GROUP * kr), 256 * (t + 1) // (GROUP * kr)) if t >= 0 else ()

        def after(t):
            scatter_core(k, dk, rc, complete(t))
            scatter_quad(k, dk, rc, rx, ry, complete(t - 2))
            if t == 8:
                scatter_quad(k, dk, rc, rx, ry, complete(7))
                scatter_quad(k, dk, rc, rx, ry, complete(8))

        return after

    def scatter_outer(k, rx, ry, rz, rw):
        for o in outer_peers + [zi]:
            wait_bytes(ry.at[o, pl.ds(0, QUAD - 1)], rs_r.at[k, 1, o])
            ry[o, qi] = rx[o, qi]
            v = ry[o, 0].astype(F32)
            for q in range(1, QUAD):
                v = v + ry[o, q].astype(F32)
            rz[o] = v.astype(BF16)
            if o is not zi:
                remote(rz.at[o], rw.at[zi], rs_s.at[k, 2], rs_r.at[k, 2, 0], dev(o, ii))

    def scatter_end(k, rz, rw):
        wait_bytes(rw.at[pl.ds(0, outer - 1)], rs_r.at[k, 2, 0])
        rw[zi] = rz[zi]
        v = rw[0].astype(F32)
        for o in range(1, outer):
            v = v + rw[o].astype(F32)
        return v

    def my_part(vector, out):
        start = me * z_.vec
        half = jnp.where(start // 128 == 0, vector[:, 0:128], vector[:, 128:256])
        half = jnp.broadcast_to(half, (8, 128))
        packed[out : out + 1, :] = pltpu.roll(half, lax.rem(128 - lax.rem(start, 128), 128), 1)[0:1, :]

    if z_.gmsg > 2 * kr:
        for dk in (dk1, dk2):
            for s in range(n):
                dk[s // GROUP, (s % GROUP) // 2, s % 2, 2 * kr :, :] = jnp.zeros((z_.gmsg - 2 * kr, 128), BF16)

    total = Sums()
    keep = keep_moments(h0, total)
    for m, count in tiles:
        out = dot(s_in[m * block : (m + count) * block, :], k0[...])
        for i in range(count):
            keep(m + i, out[i * block : (i + 1) * block, :])
    reduce_begin(0, *total.rows())
    gather_quad(1, kbuf2)
    load_cot.wait()
    g2[...] = jnp.zeros(g2.shape, F32)

    def unpack_cot(i, carry):
        here = g2.at[pl.ds(pl.multiple_of(i * block, block), block)]
        for j in range(board):
            here[pos * j : pos * j + pos, :] = cot_v[i, j].astype(F32)
        return carry

    lax.fori_loop(0, board, unpack_cot, 0)
    gather_core(0, kbuf1, outer_peers)
    gather_core(1, kbuf2, [zi])
    stats0 = bn(*reduce_end(0), gain0, shift0)

    total = Sums()
    affine1 = []
    phase(
        x0, w1, activation(h0, x0, sl0, stats0), keep_moments(h1, total),
        before=lambda: affine1.extend(gather_end(0, kbuf1, w1)),
    )
    reduce_begin(1, *total.rows())
    gather_core(1, kbuf2, outer_peers)
    k0t = jnp.transpose(k0[...])
    for t in range(9):
        mr = iota((z_.width, 128), 0)
        ml = iota((z_.width, 128), 1)
        sel = ((mr == planes * (8 - t) + ml // pos) & (ml < planes * pos)).astype(BF16)
        wtx[256 * t : 256 * t + 256, :] = dot(k0t, sel).astype(BF16)
    s_in[rows:deep, :] = jnp.zeros((deep - rows, z_.width), BF16)
    for k in range(deep // 128):
        s_t[:, 128 * k : 128 * k + 128] = jnp.transpose(s_in[128 * k : 128 * k + 128, :])
    gain2, shift2 = gather_end(1, kbuf2, w2)
    stats1 = bn(*reduce_end(1), *affine1)

    total = Sums()
    phase(x1, w2, activation(h1, x1, sl1, stats1), keep_moments(h2, total))
    reduce_begin(2, *total.rows())
    transpose_weights(w2, wt2)
    stats2 = bn(*reduce_end(2), gain2, shift2)

    total = Sums()
    inv, neg, scale, bias = stats2
    for i in range(board):
        at = part(i)
        h = h2[at, :]
        summed = h * scale + bias + x0[1, part(i, 1), :].astype(F32)
        sig = 0.5 * jnp.tanh(0.5 * summed) + 0.5
        act = summed * sig
        big[at, :] = act
        g = g2[at, :] * (sig + act * (1.0 - sig))
        g2[at, :] = g
        total.add(g, g * (h * inv + neg))
    reduce_begin(3, *total.rows())

    def pack_act(i, carry):
        v = big[pl.ds(pl.multiple_of(i * block, block), block), :]
        for j in range(board):
            act_v[i, j] = v[pos * j : pos * j + pos, :].astype(BF16)
        return carry

    lax.fori_loop(0, board, pack_act, 0)
    store_act = pltpu.make_async_copy(act_v, act_hbm, loc.at[2])
    store_act.start()
    transpose_weights(w1, wt1)
    shift_grad, gain_grad = reduce_end(3)

    total1 = Sums()

    def first_consume(i, out):
        inv, neg, _, _ = stats1
        g = out * sl1[part(i), :]
        big[part(i), :] = g
        total1.add(g, g * (h1[part(i), :] * inv + neg))

    phase(xp, wt2, pre_gradient(g2, h2, stats2, shift_grad, gain_grad), first_consume)
    reduce_begin(4, *total1.rows())
    my_part(shift_grad, z_.vec_row + 5)
    my_part(gain_grad, z_.vec_row + 4)
    kernel_grad(x1, dk2, scatter_begin(2, dk2, rc2, rx2, ry2))
    shift_grad, gain_grad = reduce_end(4)

    total0 = Sums()

    def stem_consume(i, out):
        inv, neg, _, _ = stats0
        g = (out + g2[part(i), :]) * sl0[part(i), :]
        big[part(i), :] = g
        total0.add(g, g * (h0[part(i), :] * inv + neg))

    phase(xp, wt1, pre_gradient(big, h1, stats1, shift_grad, gain_grad), stem_consume)
    reduce_begin(5, *total0.rows())
    my_part(shift_grad, z_.vec_row + 3)
    my_part(gain_grad, z_.vec_row + 2)
    kernel_grad(x0, dk1, scatter_begin(1, dk1, rc1, rx1, ry1))
    scatter_outer(2, rx2, ry2, rz2, rw2)
    shift_grad, gain_grad = reduce_end(5)

    rep_rows = jnp.concatenate([rep, jnp.zeros((128 - block, 128), BF16)], axis=0)
    rep_twice = jnp.concatenate([rep_rows, rep_rows], axis=0)
    gap = jnp.zeros((128 - block, 128), F32)

    def planes_consume(m, count, out):
        flat = []
        for i in range(count):
            v = jnp.transpose(jnp.concatenate([out[i * block : (i + 1) * block, :] * pick, gap], axis=0))
            hi = v.astype(BF16)
            flat.append(jnp.concatenate([hi, (v - hi.astype(F32)).astype(BF16)], axis=1))
        w = dot(jnp.concatenate(flat, axis=0), rep_twice)
        for i in range(count):
            for k in range(planes):
                pgrad_v[m + i, k] = w[128 * i + pos * k : 128 * i + pos * k + pos, 0:board]
        store = pltpu.make_async_copy(pgrad_v.at[pl.ds(m, count)], pgrad_hbm.at[pl.ds(m, count)], loc.at[14 + len(stores)])
        store.start()
        stores.append(store)

    stores = []

    def stem_before():
        big[0 : z_.width, :] = dot(s_t[...], xp[1, block : block + deep, :])
        for s in range(n):
            base = s * length // c_all
            dk0[s, 0:6, :] = big[base : base + 6, 0:128].astype(BF16)
            dk0[s, 6:12, :] = big[base : base + 6, 128:256].astype(BF16)
            dk0[s, 12:16, :] = jnp.zeros((4, 128), BF16)

        everyone(lambda other: remote(dk0.at[other], rw0.at[me], rs_s.at[0, 0], rs_r.at[0, 0, 0], other))

    def stem_between(k):
        if k == 1:
            scatter_outer(1, rx1, ry1, rz1, rw1)

    phase(xp, wtx, pre_gradient(big, h0, stats0, shift_grad, gain_grad, False), planes_consume, stem_between, stem_before, True)
    my_part(shift_grad, z_.vec_row + 1)
    my_part(gain_grad, z_.vec_row + 0)

    def spill(v, out):
        tmp[0 : 2 * kr, :] = v[0 : 2 * kr, :]
        packed[pl.ds(out, kr, stride=2), :] = tmp[0:kr, :]
        packed[pl.ds(out + 1, kr, stride=2), :] = tmp[kr : 2 * kr, :]

    spill(scatter_end(2, rz2, rw2), 0)
    wait_bytes(rw0.at[pl.ds(0, n - 1)], rs_r.at[0, 0, 0])
    rw0[me] = dk0[me]
    v = jnp.sum(rw0[...].astype(F32), axis=0)
    tmp[0:32, :] = jnp.zeros((32, 128), F32)
    tmp[16:32, :] = v
    left = tmp[16:22, :]
    right = tmp[22:28, :]
    tmp[pl.ds(0, 6, stride=2), :] = left
    tmp[pl.ds(1, 6, stride=2), :] = right
    flat = tmp[0:16, :]
    flat = jnp.where(off // 128 == 1, pltpu.roll(flat, 15, 0), flat)
    rolled = pltpu.roll(flat, lax.rem(128 - shift, 128), 1)
    flat = jnp.where(lane < 128 - shift, rolled, pltpu.roll(rolled, 15, 0))
    packed[z_.stem_row : z_.stem_row + 16, :] = flat
    spill(scatter_end(1, rz1, rw1), z_.first_row)

    wait_bytes(sbuf.at[pl.ds(0, outer - 1), 0], sm_s.at[0])
    wait_bytes(sbuf.at[:, pl.ds(0, GROUP - 1)], sm_s.at[1])
    for g, buf in ((0, kbuf1), (1, kbuf2)):
        wait_bytes(buf.at[pl.ds(0, outer - 1), 0, 0], kg_s.at[g, 0])
        wait_bytes(buf.at[:, pl.ds(0, QUAD - 1), 0], kg_s.at[g, 1])
        wait_bytes(buf.at[:, :, 0], kg_s.at[g, 2])
    for k in range(6):
        wait_bytes(ar_a.at[k, pl.ds(0, n - 1)], ar_s.at[k])
    wait_bytes(rw0.at[pl.ds(0, n - 1)], rs_s.at[0, 0])
    for k, rc, ry, rw in ((1, rc1, ry1, rw1), (2, rc2, ry2, rw2)):
        wait_bytes(rc, rs_s.at[k, 0])
        wait_bytes(ry.at[:, pl.ds(0, QUAD - 1)], rs_s.at[k, 1])
        wait_bytes(rw.at[pl.ds(0, outer - 1)], rs_s.at[k, 2])
    store_act.wait()
    for store in stores:
        store.wait()


def unpack_outputs(
    z_, act_in, pgrad_in, packed,
    act, pgrad, stem_kg, stem_gg, stem_sg, first_kg, first_gg, first_sg, second_kg, second_gg, second_sg, sems,
):
    copies = []
    for m in range(0, z_.board, 5):
        rows = pl.ds(m, min(5, z_.board - m))
        for src, dst in ((act_in, act), (pgrad_in, pgrad)):
            copies.append(pltpu.make_async_copy(src.at[rows], dst.at[rows], sems.at[len(copies)]))
    for copy in copies:
        copy.start()
    kr = z_.krows
    second_kg[...] = packed[0 : 2 * kr, :]
    first_kg[...] = packed[z_.first_row : z_.first_row + 2 * kr, :]
    for k, ref in enumerate((stem_gg, stem_sg, first_gg, first_sg, second_gg, second_sg)):
        ref[...] = packed[z_.vec_row + k : z_.vec_row + k + 1, 0 : z_.vec]
    flat = packed[z_.stem_row : z_.stem_row + 16, :]
    length = z_.stem_len
    for r in range(length // 128):
        stem_kg[pl.ds(128 * r, 128)] = flat[r : r + 1, :].reshape(128)
    rest = length % 128
    if rest:
        r = length // 128
        stem_kg[pl.ds(128 * r, rest)] = flat[r : r + 1, 0:rest].reshape(rest)
    for copy in copies:
        copy.wait()


def body(
    planes, history, stem_kernel, stem_gain, stem_shift, first_kernel, first_gain, first_shift,
    second_kernel, second_gain, second_shift, cotangent,
):
    n = lax.axis_size("dev")
    pt = planes.transpose(1, 3, 0, 2)
    ct = cotangent.transpose(1, 2, 0, 3)
    z_ = Sizes(n, pt.shape, ct.shape, stem_kernel.shape[0], first_kernel.shape[0])
    c, o = z_.channels, z_.outer
    lanes_k = first_kernel.shape[0] // 128

    def vm(shape, kind=F32):
        return pltpu.VMEM(shape, kind)

    def out(shape, kind=F32):
        return jax.ShapeDtypeStruct(shape, kind)

    hbm = pl.BlockSpec(memory_space=pl.ANY)
    far = pl.BlockSpec(memory_space=pltpu.HBM)
    near = pl.BlockSpec(memory_space=pltpu.VMEM)
    vec = (1, z_.vec)
    wide = (o, QUAD, 2, z_.gmsg, 128)
    scratch = [
        vm(history.shape, jnp.int32), vm(stem_kernel.shape, BF16), vm(vec, BF16), vm(vec, BF16),
        vm((lanes_k, 128), BF16), vm(vec, BF16), vm(vec, BF16), vm((lanes_k, 128), BF16), vm(vec, BF16), vm(vec, BF16),
        vm(pt.shape, BF16), vm(ct.shape, BF16), vm(ct.shape, BF16), vm(pt.shape),
        vm((z_.board * 128, 128)), vm((3, z_.tall, 128), BF16), vm((9 * 128, z_.width), BF16),
        vm((z_.deep, z_.width), BF16), vm((z_.width, z_.deep), BF16),
        vm((z_.width, c), BF16), vm((2, z_.stem_all, c)), vm((9 * c, 128), BF16),
        vm((9 * c, c), BF16), vm((9 * c, c), BF16), vm((9 * c, c), BF16), vm((9 * c, c), BF16),
        vm((3, z_.tall, c), BF16), vm((3, z_.tall, c), BF16), vm((3, z_.tall, c), BF16),
        vm((z_.rows, c)), vm((z_.rows, c)), vm((z_.rows, c)), vm((z_.rows, c)), vm((z_.rows, c)),
        vm((z_.rows, c)), vm((z_.rows, c)), vm((c, z_.deep), BF16), vm((up(2 * z_.krows + 32, 16), 128)),
        vm((o, GROUP, 16, 128), BF16), vm((o, QUAD, 2, z_.kmsg, 128), BF16), vm((o, QUAD, 2, z_.kmsg, 128), BF16),
        vm((6, n, 4, 128)),
        vm(wide, BF16), vm(wide, BF16), vm((o, QUAD, z_.gmsg, 128), BF16), vm((o, QUAD, z_.gmsg, 128), BF16),
        vm((o, QUAD, z_.gmsg, 128), BF16), vm((o, QUAD, z_.gmsg, 128), BF16),
        vm((o, QUAD, z_.gmsg, 128), BF16), vm((o, QUAD, z_.gmsg, 128), BF16),
        vm((o, z_.gmsg, 128), BF16), vm((o, z_.gmsg, 128), BF16), vm((o, z_.gmsg, 128), BF16), vm((o, z_.gmsg, 128), BF16),
        vm((n, 16, 128), BF16), vm((n, 16, 128), BF16),
        pltpu.SemaphoreType.DMA((14 + up(z_.board, 5) // 5,)), pltpu.SemaphoreType.DMA((2,)), pltpu.SemaphoreType.DMA((2,)),
        pltpu.SemaphoreType.DMA((2, 3)), pltpu.SemaphoreType.DMA((2, 3, o)),
        pltpu.SemaphoreType.DMA((6,)), pltpu.SemaphoreType.DMA((6,)),
        pltpu.SemaphoreType.DMA((3, 3)), pltpu.SemaphoreType.DMA((3, 3, o)),
    ]
    outs = pl.pallas_call(
        functools.partial(kernel, z_),
        out_shape=(out(ct.shape, BF16), out(pt.shape), out((z_.packed, 128))),
        in_specs=[far] * 12,
        out_specs=(hbm, hbm, near),
        scratch_shapes=scratch,
        compiler_params=pltpu.CompilerParams(
            collective_id=0, has_side_effects=True, vmem_limit_bytes=52 * 2**20
        ),
    )(*[
        pltpu.with_memory_space_constraint(v, pltpu.HBM)
        for v in (
            pt, ct, history, stem_kernel, stem_gain.reshape(vec), stem_shift.reshape(vec),
            first_kernel.reshape(lanes_k, 128), first_gain.reshape(vec), first_shift.reshape(vec),
            second_kernel.reshape(lanes_k, 128), second_gain.reshape(vec), second_shift.reshape(vec),
        )
    ])
    outs = pl.pallas_call(
        functools.partial(unpack_outputs, z_),
        out_shape=(
            out(ct.shape, BF16), out(pt.shape), out(stem_kernel.shape), out(vec), out(vec),
            out((lanes_k, 128)), out(vec), out(vec), out((lanes_k, 128)), out(vec), out(vec),
        ),
        in_specs=[hbm, hbm, near],
        out_specs=(hbm, hbm) + (near,) * 9,
        scratch_shapes=[pltpu.SemaphoreType.DMA((2 * up(z_.board, 5) // 5,))],
        compiler_params=pltpu.CompilerParams(vmem_limit_bytes=8 * 2**20),
    )(*outs)
    outs = list(outs)
    outs[0] = outs[0].transpose(2, 0, 1, 3)
    outs[1] = outs[1].transpose(2, 0, 3, 1)
    return tuple(outs[:2]) + tuple(v.reshape(-1) for v in outs[2:])


def solution(mesh):
    split = P("dev")
    return jax.shard_map(
        body, mesh=mesh, in_specs=(split,) * 12, out_specs=(split,) * 11, check_vma=False
    )
```

```python
import functools
import math

import jax
import jax.numpy as jnp
from jax import lax
from jax.experimental import pallas as pl
from jax.experimental.pallas import tpu as pltpu
from jax.sharding import PartitionSpec as P

F32 = jnp.float32
BF16 = jnp.bfloat16
MESH = pl.DeviceIdType.MESH
EPSILON = 1e-5
GROUP = 8
QUAD = GROUP // 2


def up(value, step):
    return -(-value // step) * step


class Sizes:
    def __init__(self, n, planes_t, cot_t, stem_len, kernel_len):
        self.n = n
        self.outer = n // GROUP
        self.board, self.planes, self.pos, _ = planes_t
        self.channels = cot_t[3]
        self.block = (self.board + 1) * self.pos
        self.live = self.board * self.pos
        self.rows = self.board * self.block
        self.deep = up(self.rows, 128)
        self.tall = 2 * self.block + self.deep
        self.taps = 9
        self.width = 256
        self.stem_len = stem_len
        self.stem_apart = 2 * stem_len >= 7 * self.channels
        self.stem_all = up(n * stem_len // self.channels, 8) + 8
        self.krows = kernel_len // self.channels
        self.kmsg = up(2 * self.krows + 4, 16)
        self.gmsg = up(2 * self.krows, 16)
        self.vec = self.channels // n
        self.first_row = up(2 * self.krows, 8)
        self.stem_row = 2 * self.first_row
        self.vec_row = self.stem_row + 16
        self.packed = self.vec_row + 8
        self.cells = n * self.pos * self.board * self.board


def iota(shape, axis):
    return lax.broadcasted_iota(jnp.int32, shape, axis)


def wait_bytes(ref, sem):
    pltpu.make_async_copy(ref, ref, sem).wait()


def dot(a, b):
    return lax.dot_general(a, b, (((1,), (0,)), ((), ())), preferred_element_type=F32)


def dot_nt(a, b):
    return lax.dot_general(a, b, (((1,), (1,)), ((), ())), preferred_element_type=F32)


def dot_tn(a, b):
    return lax.dot_general(a, b, (((0,), (0,)), ((), ())), preferred_element_type=F32)


def kernel(
    z_,
    planes_hbm, cot_hbm, hist_h, stem_kh, stem_gh, stem_sh, first_kh, first_gh, first_sh, second_kh, second_gh, second_sh,
    act_hbm, pgrad_hbm, packed,
    hist, stem_k, stem_g, stem_s, first_k, first_g, first_s, second_k, second_g, second_s,
    planes_v, cot_v, act_v, pgrad_v, y_f, vm, e_mat, s_in, s_t, k0, k0f, wtx, w1, w2, wt1, wt2,
    x0, x1, xp, h0, h1, h2, sl0, sl1, g2, big, pre_t, tmp,
    sbuf, kbuf1, kbuf2, ar_a,
    dk1, dk2, rc1, rc2, rx1, rx2, ry1, ry2, rz1, rz2, rw1, rw2,
    dk0, rw0,
    loc, sm_s, sm_r, kg_s, kg_r, ar_s, ar_r, rs_s, rs_r,
):
    n, outer, c_all = z_.n, z_.outer, z_.channels
    block, live, rows, deep = z_.block, z_.live, z_.rows, z_.deep
    board, pos, planes = z_.board, z_.pos, z_.planes
    me = lax.axis_index("dev")
    zi = me // GROUP
    ii = me % GROUP
    qi = ii // 2
    ci = ii % 2

    def dev(o, i):
        return o * GROUP + i

    def remote(src, dst, send, recv, target):
        copy = pltpu.make_async_remote_copy(
            src_ref=src, dst_ref=dst, send_sem=send, recv_sem=recv, device_id=(target,), device_id_type=MESH
        )
        copy.start()

    bits = n.bit_length() - 1
    steps = [(1 - 2 * (me // 2**b % 2)) * 2**b for b in range(bits)]

    def everyone(visit):
        for p in range(n - 1, 0, -1):
            visit(me + sum(steps[b] for b in range(bits) if p // 2**b % 2))

    outer_peers = [lax.rem(zi + k, outer) for k in range(1, outer)]
    inner_peers = [lax.rem(ii + k, GROUP) for k in range(1, GROUP)]
    quad_peers = [lax.rem(qi + k, QUAD) for k in range(1, QUAD)]
    sibling = dev(zi, qi * 2 + (1 - ci))

    loads = []
    for k, (src, dst) in enumerate((
        (stem_kh, stem_k), (stem_gh, stem_g), (stem_sh, stem_s), (first_kh, first_k), (first_gh, first_g),
        (first_sh, first_s), (second_kh, second_k), (second_gh, second_g), (second_sh, second_s), (hist_h, hist),
    )):
        copy = pltpu.make_async_copy(src, dst, loc.at[4 + k])
        copy.start()
        loads.append(copy)
    load_planes = pltpu.make_async_copy(planes_hbm, planes_v, loc.at[0])
    load_planes.start()
    load_cot = pltpu.make_async_copy(cot_hbm, cot_v, loc.at[1])
    load_cot.start()
    barrier = pltpu.get_barrier_semaphore()

    def greet(other):
        pl.semaphore_signal(barrier, inc=1, device_id=(other,), device_id_type=MESH)

    for o in outer_peers:
        greet(dev(o, ii))
    for i in inner_peers:
        greet(dev(zi, i))
    for copy in loads:
        copy.wait()
    lane = iota((16, 128), 1)
    row = iota((16, 128), 0)

    def placed(vec_ref, slot):
        tmp[0:8, :] = jnp.zeros((8, 128), F32)
        tmp[0:1, 0 : z_.vec] = vec_ref[...].astype(F32)
        start = me * z_.vec
        spread = pltpu.roll(tmp[0:8, :], lax.rem(start, 128), 1)[0:1, :]
        return jnp.where(row == slot + start // 128, spread, 0.0)

    length = z_.stem_len
    off = lax.rem(me * length, c_all)
    tmp[0:16, :] = jnp.zeros((16, 128), F32)
    for r in range(length // 128):
        tmp[r : r + 1, :] = stem_k[pl.ds(128 * r, 128)].astype(F32).reshape(1, 128)
    rest = length % 128
    if rest:
        r = length // 128
        tmp[r : r + 1, 0:rest] = stem_k[pl.ds(128 * r, rest)].astype(F32).reshape(1, rest)
    shift = lax.rem(off, 128)
    rolled = pltpu.roll(tmp[0:16, :], shift, 1)
    flat = jnp.where(lane >= shift, rolled, pltpu.roll(rolled, 1, 0))
    flat = jnp.where(off // 128 == 1, pltpu.roll(flat, 1, 0), flat)
    tmp[0:16, :] = flat
    left = tmp[pl.ds(0, 8, stride=2), :]
    right = tmp[pl.ds(1, 8, stride=2), :]
    vectors = placed(stem_g, 12) + placed(stem_s, 14)
    tmp[0:16, :] = vectors
    tmp[0:6, :] = left[0:6, :]
    tmp[6:12, :] = right[0:6, :]
    sbuf[zi, ii] = tmp[0:16, :].astype(BF16)

    kr = z_.krows

    def kernel_message(k_ref, g_ref, s_ref, buf):
        vectors = placed(g_ref, 0) + placed(s_ref, 2)
        tmp[0 : 2 * kr, :] = k_ref[...].astype(F32)
        left = tmp[pl.ds(0, kr, stride=2), :]
        right = tmp[pl.ds(1, kr, stride=2), :]
        tmp[0:kr, :] = left
        tmp[kr : 2 * kr, :] = right
        tmp[2 * kr : 2 * kr + 16, :] = vectors
        buf[zi, qi, ci] = tmp[0 : z_.kmsg, :].astype(BF16)

    kernel_message(first_k, first_g, first_s, kbuf1)

    def gather_near(g, block_o, o):
        for q in quad_peers:
            remote(block_o, block_o, kg_s.at[g, 1], kg_r.at[g, 1, o], dev(zi, q * 2 + ci))

    def gather_begin(g, buf):
        mine = buf.at[zi, qi, ci]
        for o in outer_peers:
            remote(mine, mine, kg_s.at[g, 0], kg_r.at[g, 0, zi], dev(o, ii))
        gather_near(g, mine, zi)

    def gather_quad(g, buf):
        for o in outer_peers:
            block_o = buf.at[o, qi, ci]
            wait_bytes(block_o, kg_r.at[g, 0, o])
            gather_near(g, block_o, o)

    def gather_core(g, buf):
        for o in [zi] + outer_peers:
            wait_bytes(buf.at[o, pl.ds(0, QUAD - 1), 0], kg_r.at[g, 1, o])
            remote(buf.at[o, :, ci], buf.at[o, :, ci], kg_s.at[g, 2], kg_r.at[g, 2, o], sibling)

    def gather_end(g, buf, w):
        many = 16 // math.gcd(16, kr)

        def place(p, vectors):
            there = w.at[pl.ds(pl.multiple_of(p * many * kr, 16), many * kr)]
            for d in range(many):
                s = p * many + d
                piece = buf.at[s // GROUP, (s % GROUP) // 2, s % 2]
                there[kr * d : kr * d + kr, 0:128] = piece[0:kr, :]
                there[kr * d : kr * d + kr, 128:256] = piece[kr : 2 * kr, :]
                vectors += piece[2 * kr : z_.kmsg, :].astype(F32)[0:4, :]
            return vectors

        vectors = jnp.zeros((4, 128), F32)
        for o in [zi] + outer_peers:
            wait_bytes(buf.at[o, :, 0], kg_r.at[g, 2, o])
            each = GROUP // many
            for p in range(each):
                vectors = place(o * each + p, vectors)
        return wide(vectors[0:2, :]), wide(vectors[2:4, :])

    def wide(two_rows):
        return jnp.concatenate([two_rows[0:1, :], two_rows[1:2, :]], axis=1)

    pl.semaphore_wait(barrier, outer - 1 + GROUP - 1)
    for o in outer_peers:
        remote(sbuf.at[zi, ii], sbuf.at[zi, ii], sm_s.at[0], sm_r.at[0], dev(o, ii))
    gather_begin(0, kbuf1)

    load_planes.wait()
    for i in range(board):
        y_f[i * 128 : i * 128 + 128, :] = jnp.zeros((128, 128), F32)
        for k in range(planes):
            y_f[i * 128 + pos * k : i * 128 + pos * k + pos, 0:board] = planes_v[i, k].astype(F32)
    rep = (iota((block, 128), 0) // pos == iota((block, 128), 1)).astype(BF16)
    tmp[0:8, :] = jnp.zeros((8, 128), F32)
    tmp[0:pos, 0:8] = hist[...].astype(F32)
    spread = (iota((128, 128), 1) // (2 * pos) == iota((128, 128), 0)).astype(BF16)
    present = dot(tmp[0:8, :].astype(BF16), spread)
    lane8 = iota((8, 128), 1)
    present = jnp.where(lane8 // pos == planes - 1, 1.0, present)
    present = jnp.sum(jnp.where((lane8 % pos == iota((8, 128), 0)) & (lane8 < planes * pos), present, 0.0), axis=0, keepdims=True)
    lane_b = iota((block, 128), 1)
    pick = jnp.where(lane_b % pos == iota((block, 128), 0) % pos, present, 0.0)
    wider = (iota((128, 128), 1) // pos == iota((128, 128), 0)).astype(BF16)
    for m in range(0, board, 5):
        count = min(5, board - m)
        spread_t = dot(y_f[m * 128 : (m + count) * 128, :].astype(BF16), wider)
        for i in range(count):
            v = jnp.transpose(spread_t[i * 128 : i * 128 + 128, :])[0:block, :] * pick
            at = slice((m + i + 1) * block, (m + i + 2) * block)
            vm[0, at, :] = pltpu.roll(v, pos, 0).astype(BF16)
            vm[1, at, :] = v.astype(BF16)
            vm[2, at, :] = pltpu.roll(v, block - pos, 0).astype(BF16)

    wait_bytes(sbuf.at[pl.ds(0, outer - 1), 0], sm_r.at[0])
    for i in inner_peers:
        remote(sbuf.at[:, ii], sbuf.at[:, ii], sm_s.at[1], sm_r.at[1], dev(zi, i))
    gather_quad(0, kbuf1)

    for b in range(3):
        vm[b, 0:block, :] = jnp.zeros((block, 128), BF16)
        vm[b, block + rows :, :] = jnp.zeros((z_.tall - block - rows, 128), BF16)
    for t in range(9):
        er = iota((128, z_.width), 0)
        e_mat[128 * t : 128 * t + 128, :] = (
            (iota((128, z_.width), 1) == planes * t + er // pos) & (er < planes * pos)
        ).astype(BF16)

    cuts = [0] + [min(m, board) for m in range(3, board, 6)] + [board]
    tiles = [(m, end - m) for m, end in zip(cuts, cuts[1:])]

    def taps(x, start, count):
        return jnp.concatenate([x[t % 3, start + (t // 3) * block : start + (t // 3) * block + count, :] for t in range(9)], axis=1)

    for m, count in tiles:
        s_in[m * block : (m + count) * block, :] = dot(taps(vm, m * block, count * block), e_mat[...]).astype(BF16)
    kernel_message(second_k, second_g, second_s, kbuf2)
    gather_begin(1, kbuf2)

    k0f[...] = jnp.zeros(k0f.shape, F32)

    for x in (x0, x1, xp):
        for b in range(3):
            x[b, 0:block, :] = jnp.zeros((block, c_all), BF16)
            x[b, block + rows :, :] = jnp.zeros((z_.tall - block - rows, c_all), BF16)

    wait_bytes(sbuf.at[:, pl.ds(0, GROUP - 1)], sm_r.at[1])
    vectors = jnp.zeros((4, 128), F32)
    for s in range(n):
        piece = sbuf[s // GROUP, s % GROUP].astype(F32)
        base = s * length // c_all
        apart = s % 2 if z_.stem_apart else 0
        if z_.stem_apart:
            k0f[apart, base : base + 6, 0:128] = piece[0:6, :]
            k0f[apart, base : base + 6, 128:256] = piece[6:12, :]
        else:
            k0f[0, base : base + 6, 0:128] += piece[0:6, :]
            k0f[0, base : base + 6, 128:256] += piece[6:12, :]
        vectors += piece[12:16, :]
    gain0, shift0 = wide(vectors[0:2, :]), wide(vectors[2:4, :])
    k0[...] = jnp.zeros(k0.shape, BF16)
    used = up(9 * planes, 16)
    k0[0:used, :] = (k0f[0, 0:used, :] + k0f[1, 0:used, :]).astype(BF16)

    blk_mask = iota((block, c_all), 0) < live

    def fold(v):
        return jnp.sum(v.reshape(block // 8, 8, c_all), axis=0)

    def part(i, ahead=0):
        return slice((i + ahead) * block, (i + ahead + 1) * block)

    class Sums:
        def __init__(self):
            self.a = self.b = None

        def add(self, a, b):
            a, b = fold(a), fold(b)
            self.a = a if self.a is None else self.a + a
            self.b = b if self.b is None else self.b + b

        def rows(self):
            return jnp.sum(self.a, axis=0, keepdims=True), jnp.sum(self.b, axis=0, keepdims=True)

    def phase(x, w, produce, consume, between=None, before=None, whole=False):
        done = 0
        if before is not None:
            for i in range(board):
                produce(i)
            done = board
            before()
        for k, (m, count) in enumerate(tiles):
            upto = min(board, m + count + 1)
            for i in range(done, upto):
                produce(i)
            done = max(done, upto)
            out = dot(taps(x, m * block, count * block), w[...])
            if k + 1 < len(tiles):
                upto = min(board, tiles[k + 1][0] + tiles[k + 1][1] + 1)
                for i in range(done, upto):
                    produce(i)
                done = max(done, upto)
            if whole:
                consume(m, count, out)
            else:
                for i in range(count):
                    consume(m + i, out[i * block : (i + 1) * block, :])
            if between is not None:
                between(k)

    def reduce_begin(k, a, b):
        mine = ar_a.at[k, me]
        mine[0:1, :] = a[:, 0:128]
        mine[1:2, :] = a[:, 128:256]
        mine[2:3, :] = b[:, 0:128]
        mine[3:4, :] = b[:, 128:256]

        everyone(lambda other: remote(mine, mine, ar_s.at[k], ar_r.at[k], other))

    def reduce_end(k):
        wait_bytes(ar_a.at[k, pl.ds(0, n - 1)], ar_r.at[k])
        total = jnp.sum(ar_a[k], axis=0)
        return wide(total[0:2, :]), wide(total[2:4, :])

    def bn(total, squares, gain, shift):
        centre = total * (1.0 / z_.cells)
        variance = squares * (1.0 / z_.cells) - centre * centre
        inv = lax.rsqrt(variance + EPSILON)
        scale = gain * inv
        return inv, -centre * inv, scale, shift - centre * scale

    def put(x, i, v):
        at = part(i, 1)
        x[0, at, :] = pltpu.roll(v, pos, 0).astype(BF16)
        x[1, at, :] = v.astype(BF16)
        x[2, at, :] = pltpu.roll(v, block - pos, 0).astype(BF16)

    def activation(h, x, slope, stats):
        _, _, scale, bias = stats

        def produce(i):
            v = h[part(i), :] * scale + bias
            sig = 0.5 * jnp.tanh(0.5 * v) + 0.5
            act = v * sig
            slope[part(i), :] = jnp.where(blk_mask, sig + act * (1.0 - sig), 0.0)
            put(x, i, jnp.where(blk_mask, act, 0.0))

        return produce

    def keep_moments(h, total):
        def consume(i, out):
            h[part(i), :] = out
            v = jnp.where(blk_mask, out, 0.0)
            total.add(v, v * v)

        return consume

    def pre_gradient(g, h, stats, shift_grad, gain_grad, flip=True):
        inv, neg, scale, _ = stats
        a = shift_grad * (1.0 / z_.cells)
        b = gain_grad * (1.0 / z_.cells)
        flipped = [0]

        def produce(i):
            normed = h[part(i), :] * inv + neg
            v = scale * (g[part(i), :] - a - normed * b)
            put(xp, i, jnp.where(blk_mask, v, 0.0))
            if not flip:
                return
            upto = (i + 1) * block // 128 if i + 1 < board else deep // 128
            for k in range(flipped[0], upto):
                pre_t[:, 128 * k : 128 * k + 128] = jnp.transpose(xp[1, block + 128 * k : block + 128 * k + 128, :])
            flipped[0] = upto

        return produce

    def kernel_grad(x, dk, after):
        for t in range(9):
            o = dot(pre_t[...], x[t % 3, (t // 3) * block : (t // 3) * block + deep, :])
            o = jnp.transpose(o.astype(BF16))
            r = 256 * t
            while r < 256 * t + 256:
                s, inner = r // kr, r % kr
                count = min(kr - inner, 256 * t + 256 - r)
                rows_o = o[r - 256 * t : r - 256 * t + count, :]
                here = dk.at[s // GROUP, (s % GROUP) // 2, s % 2]
                here[inner : inner + count, :] = rows_o[:, 0:128]
                here[kr + inner : kr + inner + count, :] = rows_o[:, 128:256]
                r += count
            after(t)

    def transpose_weights(w, wt):
        for t in range(9):
            wt[256 * t : 256 * t + 256, :] = jnp.transpose(w[256 * (8 - t) : 256 * (8 - t) + 256, :])

    def scatter_core(k, dk, rc, which):
        for o in which:
            remote(dk.at[o, :, 1 - ci], rc.at[o], rs_s.at[k, 0], rs_r.at[k, 0, o], sibling)

    def scatter_quad(k, dk, rc, rx, ry, which):
        for o in which:
            wait_bytes(rc.at[o], rs_r.at[k, 0, o])
            for q in range(QUAD):
                rx[o, q] = (dk[o, q, ci].astype(F32) + rc[o, q].astype(F32)).astype(BF16)
            for q in quad_peers:
                remote(rx.at[o, q], ry.at[o, qi], rs_s.at[k, 1], rs_r.at[k, 1, o], dev(zi, q * 2 + ci))

    def scatter_begin(k, dk, rc, rx, ry):
        def complete(t):
            return range(256 * t // (GROUP * kr), 256 * (t + 1) // (GROUP * kr)) if t >= 0 else ()

        def after(t):
            scatter_core(k, dk, rc, complete(t))
            scatter_quad(k, dk, rc, rx, ry, complete(t - 2))
            if t == 8:
                scatter_quad(k, dk, rc, rx, ry, complete(7))
                scatter_quad(k, dk, rc, rx, ry, complete(8))

        return after

    def scatter_outer(k, rx, ry, rz, rw):
        for o in outer_peers + [zi]:
            wait_bytes(ry.at[o, pl.ds(0, QUAD - 1)], rs_r.at[k, 1, o])
            ry[o, qi] = rx[o, qi]
            v = ry[o, 0].astype(F32)
            for q in range(1, QUAD):
                v = v + ry[o, q].astype(F32)
            rz[o] = v.astype(BF16)
            if o is not zi:
                remote(rz.at[o], rw.at[zi], rs_s.at[k, 2], rs_r.at[k, 2, 0], dev(o, ii))

    def scatter_end(k, rz, rw):
        wait_bytes(rw.at[pl.ds(0, outer - 1)], rs_r.at[k, 2, 0])
        rw[zi] = rz[zi]
        v = rw[0].astype(F32)
        for o in range(1, outer):
            v = v + rw[o].astype(F32)
        return v

    def my_part(vector, out):
        start = me * z_.vec
        half = jnp.where(start // 128 == 0, vector[:, 0:128], vector[:, 128:256])
        half = jnp.broadcast_to(half, (8, 128))
        packed[out : out + 1, :] = pltpu.roll(half, lax.rem(128 - lax.rem(start, 128), 128), 1)[0:1, :]

    if z_.gmsg > 2 * kr:
        for dk in (dk1, dk2):
            for s in range(n):
                dk[s // GROUP, (s % GROUP) // 2, s % 2, 2 * kr :, :] = jnp.zeros((z_.gmsg - 2 * kr, 128), BF16)

    total = Sums()
    keep = keep_moments(h0, total)
    for m, count in tiles:
        out = dot(s_in[m * block : (m + count) * block, :], k0[...])
        for i in range(count):
            keep(m + i, out[i * block : (i + 1) * block, :])
    reduce_begin(0, *total.rows())
    gather_core(0, kbuf1)
    load_cot.wait()
    g2[...] = jnp.zeros(g2.shape, F32)

    def unpack_cot(i, carry):
        here = g2.at[pl.ds(pl.multiple_of(i * block, block), block)]
        for j in range(board):
            here[pos * j : pos * j + pos, :] = cot_v[i, j].astype(F32)
        return carry

    lax.fori_loop(0, board, unpack_cot, 0)
    gather_quad(1, kbuf2)
    stats0 = bn(*reduce_end(0), gain0, shift0)
    gain1, shift1 = gather_end(0, kbuf1, w1)

    total = Sums()
    phase(x0, w1, activation(h0, x0, sl0, stats0), keep_moments(h1, total))
    reduce_begin(1, *total.rows())
    gather_core(1, kbuf2)
    k0t = jnp.transpose(k0[...])
    for t in range(9):
        mr = iota((z_.width, 128), 0)
        ml = iota((z_.width, 128), 1)
        sel = ((mr == planes * (8 - t) + ml // pos) & (ml < planes * pos)).astype(BF16)
        wtx[256 * t : 256 * t + 256, :] = dot(k0t, sel).astype(BF16)
    s_in[rows:deep, :] = jnp.zeros((deep - rows, z_.width), BF16)
    for k in range(deep // 128):
        s_t[:, 128 * k : 128 * k + 128] = jnp.transpose(s_in[128 * k : 128 * k + 128, :])
    gain2, shift2 = gather_end(1, kbuf2, w2)
    stats1 = bn(*reduce_end(1), gain1, shift1)

    total = Sums()
    phase(x1, w2, activation(h1, x1, sl1, stats1), keep_moments(h2, total))
    reduce_begin(2, *total.rows())
    transpose_weights(w2, wt2)
    stats2 = bn(*reduce_end(2), gain2, shift2)

    total = Sums()
    inv, neg, scale, bias = stats2
    for i in range(board):
        at = part(i)
        h = h2[at, :]
        summed = h * scale + bias + x0[1, part(i, 1), :].astype(F32)
        sig = 0.5 * jnp.tanh(0.5 * summed) + 0.5
        act = summed * sig
        big[at, :] = act
        g = g2[at, :] * (sig + act * (1.0 - sig))
        g2[at, :] = g
        total.add(g, g * (h * inv + neg))
    reduce_begin(3, *total.rows())

    def pack_act(i, carry):
        v = big[pl.ds(pl.multiple_of(i * block, block), block), :]
        for j in range(board):
            act_v[i, j] = v[pos * j : pos * j + pos, :].astype(BF16)
        return carry

    lax.fori_loop(0, board, pack_act, 0)
    store_act = pltpu.make_async_copy(act_v, act_hbm, loc.at[2])
    store_act.start()
    transpose_weights(w1, wt1)
    shift_grad, gain_grad = reduce_end(3)

    total1 = Sums()

    def first_consume(i, out):
        inv, neg, _, _ = stats1
        g = out * sl1[part(i), :]
        big[part(i), :] = g
        total1.add(g, g * (h1[part(i), :] * inv + neg))

    phase(xp, wt2, pre_gradient(g2, h2, stats2, shift_grad, gain_grad), first_consume)
    reduce_begin(4, *total1.rows())
    my_part(shift_grad, z_.vec_row + 5)
    my_part(gain_grad, z_.vec_row + 4)
    kernel_grad(x1, dk2, scatter_begin(2, dk2, rc2, rx2, ry2))
    shift_grad, gain_grad = reduce_end(4)

    total0 = Sums()

    def stem_consume(i, out):
        inv, neg, _, _ = stats0
        g = (out + g2[part(i), :]) * sl0[part(i), :]
        big[part(i), :] = g
        total0.add(g, g * (h0[part(i), :] * inv + neg))

    phase(xp, wt1, pre_gradient(big, h1, stats1, shift_grad, gain_grad), stem_consume)
    reduce_begin(5, *total0.rows())
    my_part(shift_grad, z_.vec_row + 3)
    my_part(gain_grad, z_.vec_row + 2)
    kernel_grad(x0, dk1, scatter_begin(1, dk1, rc1, rx1, ry1))
    scatter_outer(2, rx2, ry2, rz2, rw2)
    shift_grad, gain_grad = reduce_end(5)

    rep_rows = jnp.concatenate([rep, jnp.zeros((128 - block, 128), BF16)], axis=0)
    rep_twice = jnp.concatenate([rep_rows, rep_rows], axis=0)
    gap = jnp.zeros((128 - block, 128), F32)

    def planes_consume(m, count, out):
        flat = []
        for i in range(count):
            v = jnp.transpose(jnp.concatenate([out[i * block : (i + 1) * block, :] * pick, gap], axis=0))
            hi = v.astype(BF16)
            flat.append(jnp.concatenate([hi, (v - hi.astype(F32)).astype(BF16)], axis=1))
        w = dot(jnp.concatenate(flat, axis=0), rep_twice)
        for i in range(count):
            for k in range(planes):
                pgrad_v[m + i, k] = w[128 * i + pos * k : 128 * i + pos * k + pos, 0:board]
        store = pltpu.make_async_copy(pgrad_v.at[pl.ds(m, count)], pgrad_hbm.at[pl.ds(m, count)], loc.at[14 + len(stores)])
        store.start()
        stores.append(store)

    stores = []

    def stem_before():
        big[0 : z_.width, :] = dot(s_t[...], xp[1, block : block + deep, :])
        for s in range(n):
            base = s * length // c_all
            dk0[s, 0:6, :] = big[base : base + 6, 0:128].astype(BF16)
            dk0[s, 6:12, :] = big[base : base + 6, 128:256].astype(BF16)
            dk0[s, 12:16, :] = jnp.zeros((4, 128), BF16)

        everyone(lambda other: remote(dk0.at[other], rw0.at[me], rs_s.at[0, 0], rs_r.at[0, 0, 0], other))

    def stem_between(k):
        if k == 1:
            scatter_outer(1, rx1, ry1, rz1, rw1)

    phase(xp, wtx, pre_gradient(big, h0, stats0, shift_grad, gain_grad, False), planes_consume, stem_between, stem_before, True)
    my_part(shift_grad, z_.vec_row + 1)
    my_part(gain_grad, z_.vec_row + 0)

    def spill(v, out):
        tmp[0 : 2 * kr, :] = v[0 : 2 * kr, :]
        packed[pl.ds(out, kr, stride=2), :] = tmp[0:kr, :]
        packed[pl.ds(out + 1, kr, stride=2), :] = tmp[kr : 2 * kr, :]

    spill(scatter_end(2, rz2, rw2), 0)
    wait_bytes(rw0.at[pl.ds(0, n - 1)], rs_r.at[0, 0, 0])
    rw0[me] = dk0[me]
    v = jnp.sum(rw0[...].astype(F32), axis=0)
    tmp[0:32, :] = jnp.zeros((32, 128), F32)
    tmp[16:32, :] = v
    left = tmp[16:22, :]
    right = tmp[22:28, :]
    tmp[pl.ds(0, 6, stride=2), :] = left
    tmp[pl.ds(1, 6, stride=2), :] = right
    flat = tmp[0:16, :]
    flat = jnp.where(off // 128 == 1, pltpu.roll(flat, 15, 0), flat)
    rolled = pltpu.roll(flat, lax.rem(128 - shift, 128), 1)
    flat = jnp.where(lane < 128 - shift, rolled, pltpu.roll(rolled, 15, 0))
    packed[z_.stem_row : z_.stem_row + 16, :] = flat
    spill(scatter_end(1, rz1, rw1), z_.first_row)

    wait_bytes(sbuf.at[pl.ds(0, outer - 1), 0], sm_s.at[0])
    wait_bytes(sbuf.at[:, pl.ds(0, GROUP - 1)], sm_s.at[1])
    for g, buf in ((0, kbuf1), (1, kbuf2)):
        wait_bytes(buf.at[pl.ds(0, outer - 1), 0, 0], kg_s.at[g, 0])
        wait_bytes(buf.at[:, pl.ds(0, QUAD - 1), 0], kg_s.at[g, 1])
        wait_bytes(buf.at[:, :, 0], kg_s.at[g, 2])
    for k in range(6):
        wait_bytes(ar_a.at[k, pl.ds(0, n - 1)], ar_s.at[k])
    wait_bytes(rw0.at[pl.ds(0, n - 1)], rs_s.at[0, 0])
    for k, rc, ry, rw in ((1, rc1, ry1, rw1), (2, rc2, ry2, rw2)):
        wait_bytes(rc, rs_s.at[k, 0])
        wait_bytes(ry.at[:, pl.ds(0, QUAD - 1)], rs_s.at[k, 1])
        wait_bytes(rw.at[pl.ds(0, outer - 1)], rs_s.at[k, 2])
    store_act.wait()
    for store in stores:
        store.wait()


def unpack_outputs(
    z_, act_in, pgrad_in, packed,
    act, pgrad, stem_kg, stem_gg, stem_sg, first_kg, first_gg, first_sg, second_kg, second_gg, second_sg,
    stem_v, g0, s0, g1, s1, g2, s2, sems,
):
    copies = []

    def send(src, dst):
        copies.append(pltpu.make_async_copy(src, dst, sems.at[len(copies)]))
        copies[-1].start()

    for m in range(0, z_.board, 5):
        rows = pl.ds(m, min(5, z_.board - m))
        send(act_in.at[rows], act.at[rows])
        send(pgrad_in.at[rows], pgrad.at[rows])
    kr = z_.krows
    send(packed.at[pl.ds(0, 2 * kr)], second_kg)
    send(packed.at[pl.ds(z_.first_row, 2 * kr)], first_kg)
    flat = packed[z_.stem_row : z_.stem_row + 16, :]
    length = z_.stem_len
    for r in range(length // 128):
        stem_v[pl.ds(128 * r, 128)] = flat[r : r + 1, :].reshape(128)
    rest = length % 128
    if rest:
        r = length // 128
        stem_v[pl.ds(128 * r, rest)] = flat[r : r + 1, 0:rest].reshape(rest)
    send(stem_v, stem_kg)
    pairs = ((g0, stem_gg), (s0, stem_sg), (g1, first_gg), (s1, first_sg), (g2, second_gg), (s2, second_sg))
    for k, (here, out) in enumerate(pairs):
        here[...] = packed[z_.vec_row + k : z_.vec_row + k + 1, 0 : z_.vec]
        send(here, out)
    for copy in copies:
        copy.wait()


def body(
    planes, history, stem_kernel, stem_gain, stem_shift, first_kernel, first_gain, first_shift,
    second_kernel, second_gain, second_shift, cotangent,
):
    n = lax.axis_size("dev")
    pt = planes.transpose(1, 3, 0, 2)
    ct = cotangent.transpose(1, 2, 0, 3)
    z_ = Sizes(n, pt.shape, ct.shape, stem_kernel.shape[0], first_kernel.shape[0])
    c, o = z_.channels, z_.outer
    lanes_k = first_kernel.shape[0] // 128

    def vm(shape, kind=F32):
        return pltpu.VMEM(shape, kind)

    def out(shape, kind=F32):
        return jax.ShapeDtypeStruct(shape, kind)

    hbm = pl.BlockSpec(memory_space=pl.ANY)
    far = pl.BlockSpec(memory_space=pltpu.HBM)
    near = pl.BlockSpec(memory_space=pltpu.VMEM)
    vec = (1, z_.vec)
    wide = (o, QUAD, 2, z_.gmsg, 128)
    scratch = [
        vm(history.shape, jnp.int32), vm(stem_kernel.shape, BF16), vm(vec, BF16), vm(vec, BF16),
        vm((lanes_k, 128), BF16), vm(vec, BF16), vm(vec, BF16), vm((lanes_k, 128), BF16), vm(vec, BF16), vm(vec, BF16),
        vm(pt.shape, BF16), vm(ct.shape, BF16), vm(ct.shape, BF16), vm(pt.shape),
        vm((z_.board * 128, 128)), vm((3, z_.tall, 128), BF16), vm((9 * 128, z_.width), BF16),
        vm((z_.deep, z_.width), BF16), vm((z_.width, z_.deep), BF16),
        vm((z_.width, c), BF16), vm((2, z_.stem_all, c)), vm((9 * c, 128), BF16),
        vm((9 * c, c), BF16), vm((9 * c, c), BF16), vm((9 * c, c), BF16), vm((9 * c, c), BF16),
        vm((3, z_.tall, c), BF16), vm((3, z_.tall, c), BF16), vm((3, z_.tall, c), BF16),
        vm((z_.rows, c)), vm((z_.rows, c)), vm((z_.rows, c)), vm((z_.rows, c)), vm((z_.rows, c)),
        vm((z_.rows, c)), vm((z_.rows, c)), vm((c, z_.deep), BF16), vm((up(2 * z_.krows + 32, 16), 128)),
        vm((o, GROUP, 16, 128), BF16), vm((o, QUAD, 2, z_.kmsg, 128), BF16), vm((o, QUAD, 2, z_.kmsg, 128), BF16),
        vm((6, n, 4, 128)),
        vm(wide, BF16), vm(wide, BF16), vm((o, QUAD, z_.gmsg, 128), BF16), vm((o, QUAD, z_.gmsg, 128), BF16),
        vm((o, QUAD, z_.gmsg, 128), BF16), vm((o, QUAD, z_.gmsg, 128), BF16),
        vm((o, QUAD, z_.gmsg, 128), BF16), vm((o, QUAD, z_.gmsg, 128), BF16),
        vm((o, z_.gmsg, 128), BF16), vm((o, z_.gmsg, 128), BF16), vm((o, z_.gmsg, 128), BF16), vm((o, z_.gmsg, 128), BF16),
        vm((n, 16, 128), BF16), vm((n, 16, 128), BF16),
        pltpu.SemaphoreType.DMA((14 + up(z_.board, 5) // 5,)), pltpu.SemaphoreType.DMA((2,)), pltpu.SemaphoreType.DMA((2,)),
        pltpu.SemaphoreType.DMA((2, 3)), pltpu.SemaphoreType.DMA((2, 3, o)),
        pltpu.SemaphoreType.DMA((6,)), pltpu.SemaphoreType.DMA((6,)),
        pltpu.SemaphoreType.DMA((3, 3)), pltpu.SemaphoreType.DMA((3, 3, o)),
    ]
    outs = pl.pallas_call(
        functools.partial(kernel, z_),
        out_shape=(out(ct.shape, BF16), out(pt.shape), out((z_.packed, 128))),
        in_specs=[far] * 12,
        out_specs=(hbm, hbm, near),
        scratch_shapes=scratch,
        compiler_params=pltpu.CompilerParams(
            collective_id=0, has_side_effects=True, vmem_limit_bytes=52 * 2**20
        ),
    )(*[
        pltpu.with_memory_space_constraint(v, pltpu.HBM)
        for v in (
            pt, ct, history, stem_kernel, stem_gain.reshape(vec), stem_shift.reshape(vec),
            first_kernel.reshape(lanes_k, 128), first_gain.reshape(vec), first_shift.reshape(vec),
            second_kernel.reshape(lanes_k, 128), second_gain.reshape(vec), second_shift.reshape(vec),
        )
    ])
    outs = pl.pallas_call(
        functools.partial(unpack_outputs, z_),
        out_shape=(
            out(ct.shape, BF16), out(pt.shape), out(stem_kernel.shape), out(vec), out(vec),
            out((lanes_k, 128)), out(vec), out(vec), out((lanes_k, 128)), out(vec), out(vec),
        ),
        in_specs=[hbm, hbm, near],
        out_specs=(hbm,) * 11,
        scratch_shapes=[vm(stem_kernel.shape)] + [vm(vec)] * 6 + [pltpu.SemaphoreType.DMA((2 * up(z_.board, 5) // 5 + 9,))],
        compiler_params=pltpu.CompilerParams(vmem_limit_bytes=8 * 2**20),
    )(*outs)
    outs = list(outs)
    outs[0] = outs[0].transpose(2, 0, 1, 3)
    outs[1] = outs[1].transpose(2, 0, 3, 1)
    return tuple(outs[:2]) + tuple(v.reshape(-1) for v in outs[2:])


def solution(mesh):
    split = P("dev")
    return jax.shard_map(
        body, mesh=mesh, in_specs=(split,) * 12, out_specs=(split,) * 11, check_vma=False
    )
```
